128 devices in a mesh: walker: 16 (over x, y_hi, core), prow: 2 (over y_lo), pcol: 4 (over z).
Axes of the slice: x: 4, y: 4 (y_hi: 2, y_lo: 2; y = y_hi * 2 + y_lo), z: 4, core: 2. Of those that a mesh axis runs over, the one named last changes fastest.
Arguments:
- o_rows: bfloat16 [32768, 2048], P('walker', ('prow', 'pcol')), may hold values from -21 to 21
- o_cols: bfloat16 [32768, 4096], P('walker', ('pcol', 'prow')), may hold values from -48 to 48
- grad_energy: bfloat16 [32768, 4096], P('walker', ('pcol', 'prow')), may hold values from -8 to 8
- energy: float32 [32768], P('walker'), may hold values from -5 to 1
Outputs:
- hamil: float32 [2048, 4096], P(('prow', 'walker'), 'pcol')
- correlation: float32 [2048, 4096], P(('prow', 'walker'), 'pcol')
The draws below stay inside these ranges and needn't reach their ends.
All inputs are finite; a program needn't handle non-finite values.
Results may differ from the reference program's by a relative error of at most 0.008.
Values may be sent and summed in bfloat16 or wider, within the bound.
A program may use at most 128 MiB of HBM per device.

```python
import jax
import jax.numpy as jnp
from jax import lax

SAMPLES = 32768
ROWS = 2048
NCOL = 4096


def noise_field(key, shape):
    return jnp.clip(jax.random.normal(key, shape, jnp.float32), -4.0, 4.0)


def sample_scale():
    return 0.5 + jnp.arange(SAMPLES, dtype=jnp.float32) / SAMPLES


def offsets(key, count):
    return jax.random.uniform(key, (count,), jnp.float32, -2.0, 2.0)


def col_scales(key, count):
    return jnp.exp(jax.random.uniform(key, (count,), jnp.float32, jnp.log(0.3), jnp.log(3.0)))


def shared_base(key):
    return noise_field(jax.random.fold_in(key, 1), (SAMPLES, ROWS))


def tiled_base(key):
    return jnp.tile(shared_base(key), (1, NCOL // ROWS))


def draw_o_rows(key, part):
    base = shared_base(key)
    shift = offsets(jax.random.fold_in(key, 2), ROWS)
    spread = col_scales(jax.random.fold_in(key, 3), ROWS)
    values = sample_scale()[:, None] * (shift + spread * base)
    return values.astype(jnp.bfloat16)


def draw_o_cols(key, part):
    tiled = tiled_base(key)
    mixing = jax.random.uniform(jax.random.fold_in(key, 4), (NCOL,), jnp.float32, 0.5, 1.5)
    own_part = noise_field(jax.random.fold_in(key, 5), (SAMPLES, NCOL))
    spread = col_scales(jax.random.fold_in(key, 6), NCOL)
    shift = offsets(jax.random.fold_in(key, 7), NCOL)
    values = sample_scale()[:, None] * (shift + spread * (mixing * tiled + own_part))
    return values.astype(jnp.bfloat16)


def draw_grad_energy(key, part):
    tiled = tiled_base(key)
    factor = jax.random.uniform(jax.random.fold_in(key, 8), (NCOL,), jnp.float32, 0.5, 1.5)
    extra = noise_field(jax.random.fold_in(key, 9), (SAMPLES, NCOL))
    return (factor * tiled + 0.5 * extra).astype(jnp.bfloat16)


def draw_energy(key, part):
    extra = noise_field(jax.random.fold_in(key, 10), (SAMPLES,))
    return -(0.5 + 1.5 * sample_scale()) + 0.5 * extra


def setup_inputs(seed: int = 0) -> dict:
    key_list = jax.random.split(jax.random.key(seed), 5)
    o_rows = draw_o_rows(jax.random.fold_in(key_list[4], 71), 0)
    o_cols = draw_o_cols(jax.random.fold_in(key_list[4], 71), 0)
    grad_energy = draw_grad_energy(jax.random.fold_in(key_list[4], 71), 0)
    energy = draw_energy(jax.random.fold_in(key_list[4], 71), 0)
    return dict(o_rows=o_rows, o_cols=o_cols, grad_energy=grad_energy, energy=energy)


def reference(o_rows, o_cols, grad_energy, energy):
    row_mean = jnp.sum(o_rows.astype(jnp.float32), axis=0) / SAMPLES
    col_mean = jnp.sum(o_cols.astype(jnp.float32), axis=0) / SAMPLES
    d_rows = (o_rows.astype(jnp.float32) - row_mean).astype(jnp.bfloat16)
    d_cols = (o_cols.astype(jnp.float32) - col_mean).astype(jnp.bfloat16)
    weighted = (energy[:, None] * d_cols.astype(jnp.float32) + grad_energy.astype(jnp.float32)).astype(jnp.bfloat16)
    dims = (((0,), (0,)), ((), ()))
    correlation = lax.dot_general(d_rows, d_cols, dims, preferred_element_type=jnp.float32) / SAMPLES
    hamil = lax.dot_general(d_rows, weighted, dims, preferred_element_type=jnp.float32) / SAMPLES
    return hamil, correlation
```

```python
import functools

import jax
import jax.numpy as jnp
from jax import lax
from jax.experimental import pallas as pl
from jax.experimental.pallas import tpu as pltpu
from jax.sharding import PartitionSpec as P

MESH = pl.DeviceIdType.MESH
F32 = jnp.float32
BF16 = jnp.bfloat16

CHUNKS = [
    (0, 0, 0), (0, 0, 1),
    (0, 3, 0), (0, 1, 0), (1, 0, 0),
    (0, 1, 1), (0, 3, 1), (1, 0, 1),
    (0, 2, 0), (0, 2, 1),
    (1, 3, 0), (1, 1, 0), (1, 2, 0),
    (1, 2, 1), (1, 3, 1), (1, 1, 1),
]
LAG = 3


def kernel(
    samples_total,
    r_hbm, c_hbm, g_hbm, e_ref,
    hamil_ref, corr_ref,
    rbuf, cbuf, gbuf, cw, rt, part, csend, crecv, xsend, xown, xrecv, ysend, yrecv,
    mown, mcore, mchip, mrecv, rmean,
    load_sem, rsend_sem, rrecv_sem, msend_sem, mrecv_sem,
    csend_sem, crecv_sem, xsend_sem, xrecv_sem, ysend_sem, yrecv_sem,
):
    w = lax.axis_index("walker")
    p = lax.axis_index("prow")
    q = lax.axis_index("pcol")
    x = w // 4
    yh = lax.rem(w // 2, 2)
    c = lax.rem(w, 2)
    samples, ncols = c_hbm.shape
    width = 2 * ncols

    def device(dx=0, dyh=0, dc=0, dp=0, dz=0):
        xx = lax.rem(x + dx, 4)
        yy = lax.rem(yh + dyh, 2)
        core = lax.rem(c + dc, 2)
        return {
            "walker": (xx * 2 + yy) * 2 + core,
            "prow": lax.rem(p + dp, 2),
            "pcol": lax.rem(q + dz, 4),
        }

    partners = [device(dc=1)]
    partners += [device(dx=a, dyh=b) for a in range(4) for b in range(2) if a or b]
    partners += [device(dp=a, dz=b) for a in range(2) for b in range(4) if a or b]
    partners += [device(dyh=1, dp=1)]
    barrier = pltpu.get_barrier_semaphore()
    for other in partners:
        pl.semaphore_signal(barrier, inc=1, device_id=other, device_id_type=MESH)

    loads = []
    for h in range(2):
        loads.append(pltpu.make_async_copy(
            r_hbm.at[:, pl.ds(128 * h, 128)], rbuf.at[0, 0, h], load_sem.at[h]))
    loads.append(pltpu.make_async_copy(c_hbm, cbuf, load_sem.at[2]))
    loads.append(pltpu.make_async_copy(g_hbm, gbuf, load_sem.at[3]))
    for copy in loads:
        copy.start()
    pl.semaphore_wait(barrier, len(partners))

    started = []

    def send(src, dst, ssem, rsem, target):
        copy = pltpu.make_async_remote_copy(
            src_ref=src, dst_ref=dst, send_sem=ssem, recv_sem=rsem,
            device_id=target, device_id_type=MESH)
        copy.start()
        return copy

    def send_rows(src_slot, dst_slot, number, dp=0, dz=0):
        a, d, h = src_slot
        started.append(send(
            rbuf.at[a, d, h], rbuf.at[dst_slot[0], dst_slot[1], dst_slot[2]],
            rsend_sem.at[number], rrecv_sem.at[dst_slot[0], dst_slot[1], dst_slot[2]],
            device(dp=dp, dz=dz)))

    arrived = set()

    def wait_rows(a, d, h):
        if (a, d, h) in arrived or (a, d) == (0, 0):
            return
        arrived.add((a, d, h))
        pltpu.make_async_remote_copy(
            src_ref=rbuf.at[a, d, h], dst_ref=rbuf.at[a, d, h],
            send_sem=rsend_sem.at[0], recv_sem=rrecv_sem.at[a, d, h],
            device_id=device(dz=1), device_id_type=MESH).wait_recv()

    for h in range(2):
        loads[h].wait()
        send_rows((0, 0, h), (0, 3, h), 3 * h, dz=1)
        send_rows((0, 0, h), (0, 1, h), 3 * h + 1, dz=3)
        send_rows((0, 0, h), (1, 0, h), 3 * h + 2, dp=1)

    mown[...] = jnp.zeros_like(mown)

    def block_sums(ref, lanes):
        def body(i, acc):
            values = ref[pl.ds(pl.multiple_of(i * 128, 128), 128), :].astype(F32)
            return acc + jnp.sum(values.reshape(16, 8, lanes), axis=0)
        acc = lax.fori_loop(0, samples // 128, body, jnp.zeros((8, lanes), F32))
        return jnp.sum(acc, axis=0, keepdims=True)

    for h in range(2):
        mown[h:h + 1, :] = block_sums(rbuf.at[0, 0, h], 128)
    loads[2].wait()
    csum = block_sums(cbuf, ncols)
    for k in range(ncols // 128):
        mown[2 + k:3 + k, :] = csum[:, 128 * k:128 * (k + 1)]

    copy = send(mown, mcore, msend_sem.at[0], mrecv_sem.at[0], device(dc=1))
    copy.wait_recv()
    started.append(copy)
    mchip[0] = mown[...] + mcore[...]
    copies = []
    for dx in range(4):
        for dyh in range(2):
            j = dx * 2 + dyh
            if j:
                copies.append(send(
                    mchip.at[0], mrecv.at[j], msend_sem.at[j], mrecv_sem.at[j], device(dx=dx, dyh=dyh)))
    loads[3].wait()
    total = mchip[0]
    for j, copy in enumerate(copies):
        copy.wait_recv()
        total = total + mrecv[j + 1]
    started += copies
    rmean[0, 0] = total * (1.0 / samples_total)
    mean_copies = []
    for a in range(2):
        for b in range(4):
            if a or b:
                j = 7 + a * 4 + b
                mean_copies.append(send(
                    rmean.at[0, 0], rmean.at[a, (4 - b) % 4],
                    msend_sem.at[j], mrecv_sem.at[j], device(dp=a, dz=b)))

    col_mean = jnp.concatenate([rmean[0, 0, 2 + k:3 + k, :] for k in range(ncols // 128)], axis=1)

    def build(i, _):
        rows = pl.ds(pl.multiple_of(i * 128, 128), 128)
        d_cols = (cbuf[rows, :].astype(F32) - col_mean).astype(BF16)
        cw[rows, pl.ds(0, ncols)] = d_cols
        energy = jnp.broadcast_to(e_ref[pl.ds(i, 1), :], (128, 128)).T
        energy = jnp.concatenate([energy] * (ncols // 128), axis=1)
        weighted = energy * d_cols.astype(F32) + gbuf[rows, :].astype(F32)
        cw[rows, pl.ds(ncols, ncols)] = weighted.astype(BF16)
        return 0

    lax.fori_loop(0, samples // 128, build, 0)

    for copy in mean_copies:
        copy.wait_recv()
    started += mean_copies

    def after_wait(chunk):
        if chunk == (0, 3, 0):
            send_rows((0, 3, 0), (0, 2, 0), 6, dz=1)
        if chunk == (0, 1, 1):
            send_rows((0, 1, 1), (0, 2, 1), 7, dz=3)
        if chunk == (0, 2, 0):
            send_rows((0, 2, 0), (1, 2, 0), 12, dp=1)
        if chunk == (0, 2, 1):
            send_rows((0, 2, 1), (1, 2, 1), 13, dp=1)

    def before(i):
        if i == 6:
            for h in range(2):
                wait_rows(1, 0, h)
                send_rows((1, 0, h), (1, 3, h), 8 + 2 * h, dz=1)
                send_rows((1, 0, h), (1, 1, h), 9 + 2 * h, dz=3)

    core_copies = {}
    half = 64

    def multiply(i):
        chunk = a, d, h = CHUNKS[i]
        wait_rows(a, d, h)
        after_wait(chunk)
        before(i)
        mean = rmean[a, d, h:h + 1, :]

        def center(k, _):
            rows = pl.ds(pl.multiple_of(k * 256, 256), 256)
            values = rbuf[a, d, h, rows, :].astype(F32) - mean
            rt[:, rows] = values.T.astype(BF16)
            return 0

        lax.fori_loop(0, samples // 256, center, 0)

        def product(n, _):
            cols = pl.ds(pl.multiple_of(n * 256, 256), 256)
            tile = jnp.dot(rt[...], cw[:, cols], preferred_element_type=F32)
            part[i % 2, :, cols] = tile
            csend[i, :, cols] = tile.astype(BF16)
            return 0

        lax.fori_loop(0, width // 256, product, 0)
        other = pl.ds(pl.multiple_of(half * (1 - c), half), half)
        core_copies[i] = send(
            csend.at[i, other], crecv.at[i], csend_sem.at[i], crecv_sem.at[i], device(dc=1))
        started.append(core_copies[i])

    def x_target(i):
        return lax.rem(q + CHUNKS[i][1], 4)

    def x_copy(i):
        a, d, h = CHUNKS[i]
        hop = lax.rem(x_target(i) + 4 - x, 4)
        return pltpu.make_async_remote_copy(
            src_ref=xsend.at[i], dst_ref=xrecv.at[2 * a + h, hop - 1],
            send_sem=xsend_sem.at[i], recv_sem=xrecv_sem.at[2 * a + h, hop - 1],
            device_id=device(dx=hop), device_id_type=MESH)

    def chip_sum(i):
        a, d, h = CHUNKS[i]
        core_copies[i].wait_recv()
        mine = pl.ds(pl.multiple_of(half * c, half), half)
        value = part[i % 2, mine, :] + crecv[i].astype(F32)
        away = x_target(i) != x

        @pl.when(away)
        def _():
            xsend[i] = value.astype(BF16)
            x_copy(i).start()

        @pl.when(jnp.logical_not(away))
        def _():
            xown[2 * a + h] = value

    def y_copy(a, h):
        y = 2 * yh + p
        return pltpu.make_async_remote_copy(
            src_ref=ysend.at[2 * a + h], dst_ref=yrecv.at[y],
            send_sem=ysend_sem.at[2 * a + h], recv_sem=yrecv_sem.at[y],
            device_id=device(dyh=h + 2 - yh, dp=a), device_id_type=MESH)

    def x_sum(i):
        a, d, h = CHUNKS[i]
        k = 2 * a + h

        @pl.when(x_target(i) == x)
        def _():
            value = xown[k]
            for hop in range(3):
                pltpu.make_async_remote_copy(
                    src_ref=xsend.at[i], dst_ref=xrecv.at[k, hop],
                    send_sem=xsend_sem.at[i], recv_sem=xrecv_sem.at[k, hop],
                    device_id=device(dx=1), device_id_type=MESH).wait_recv()
                value = value + xrecv[k, hop].astype(F32)
            if a == 0:
                @pl.when(yh == h)
                def _():
                    yrecv[2 * yh + p] = value.astype(BF16)

                @pl.when(yh != h)
                def _():
                    ysend[k] = value.astype(BF16)
                    y_copy(a, h).start()
            else:
                ysend[k] = value.astype(BF16)
                y_copy(a, h).start()

    count = len(CHUNKS)
    for i in range(count + LAG):
        if i < count:
            multiply(i)
        if 1 <= i <= count:
            chip_sum(i - 1)
        if i >= LAG:
            x_sum(i - LAG)

    for source in range(4):
        @pl.when(source != 2 * yh + p)
        def _():
            pltpu.make_async_remote_copy(
                src_ref=ysend.at[0], dst_ref=yrecv.at[source],
                send_sem=ysend_sem.at[0], recv_sem=yrecv_sem.at[source],
                device_id=device(dp=1), device_id_type=MESH).wait_recv()
    for part_p in range(2):
        value = yrecv[part_p].astype(F32) + yrecv[2 + part_p].astype(F32)
        cols = pl.ds(part_p * ncols, ncols)
        corr_ref[:, cols] = value[:, :ncols]
        hamil_ref[:, cols] = value[:, ncols:]

    for copy in started:
        copy.wait_send()
    for i in range(count):
        @pl.when(x_target(i) != x)
        def _(i=i):
            x_copy(i).wait_send()
    for a in range(2):
        for h in range(2):
            if a:
                y_copy(a, h).wait_send()
            else:
                @pl.when(yh != h)
                def _(a=a, h=h):
                    y_copy(a, h).wait_send()


def per_device(o_rows, o_cols, grad_energy, energy):
    samples, nrows = o_rows.shape
    ncols = o_cols.shape[1]
    width = 2 * ncols
    total = samples * lax.axis_size("walker")
    dma = pltpu.SemaphoreType.DMA
    out = jax.ShapeDtypeStruct((64, width), F32)
    hamil, corr = pl.pallas_call(
        functools.partial(kernel, total),
        name="tiles",
        out_shape=(out, out),
        in_specs=[pl.BlockSpec(memory_space=pl.ANY)] * 3 + [pl.BlockSpec(memory_space=pltpu.VMEM)],
        out_specs=(pl.BlockSpec(memory_space=pltpu.VMEM),) * 2,
        scratch_shapes=[
            pltpu.VMEM((2, 4, 2, samples, 128), BF16),
            pltpu.VMEM((samples, ncols), BF16),
            pltpu.VMEM((samples, ncols), BF16),
            pltpu.VMEM((samples, width), BF16),
            pltpu.VMEM((128, samples), BF16),
            pltpu.VMEM((2, 128, width), F32),
            pltpu.VMEM((16, 128, width), BF16),
            pltpu.VMEM((16, 64, width), BF16),
            pltpu.VMEM((16, 64, width), BF16),
            pltpu.VMEM((4, 64, width), F32),
            pltpu.VMEM((4, 3, 64, width), BF16),
            pltpu.VMEM((4, 64, width), BF16),
            pltpu.VMEM((4, 64, width), BF16),
            pltpu.VMEM((8, 128), F32),
            pltpu.VMEM((8, 128), F32),
            pltpu.VMEM((1, 8, 128), F32),
            pltpu.VMEM((8, 8, 128), F32),
            pltpu.VMEM((2, 4, 8, 128), F32),
            dma((4,)), dma((14,)), dma((2, 4, 2)), dma((15,)), dma((15,)),
            dma((16,)), dma((16,)), dma((16,)), dma((4, 3)), dma((4,)), dma((4,)),
        ],
        compiler_params=pltpu.CompilerParams(
            collective_id=0, has_side_effects=True, vmem_limit_bytes=56 * 2**20),
        cost_estimate=pl.CostEstimate(
            flops=2 * samples * 2048 * width, bytes_accessed=6 * 2**20, transcendentals=0),
    )(o_rows, o_cols, grad_energy, energy.reshape(samples // 128, 128))
    scale = 1.0 / total
    return hamil * scale, corr * scale


def solution(mesh):
    in_specs = (
        P("walker", ("prow", "pcol")),
        P("walker", ("pcol", "prow")),
        P("walker", ("pcol", "prow")),
        P("walker"),
    )
    out_specs = (P(("prow", "walker"), "pcol"), P(("prow", "walker"), "pcol"))
    return jax.shard_map(
        per_device, mesh=mesh, in_specs=in_specs, out_specs=out_specs, check_vma=False
    )
```

```python
import functools

import jax
import jax.numpy as jnp
from jax import lax
from jax.experimental import pallas as pl
from jax.experimental.pallas import tpu as pltpu
from jax.sharding import PartitionSpec as P

MESH = pl.DeviceIdType.MESH
F32 = jnp.float32
BF16 = jnp.bfloat16

GROUPS = [
    [(0, 0, 0), (0, 0, 1)],
    [(0, 3, 0), (0, 1, 1), (1, 0, 0)],
    [(0, 3, 1), (0, 1, 0), (1, 0, 1)],
    [(0, 2, 0), (0, 2, 1)],
    [(1, 3, 0), (1, 1, 0), (1, 2, 0)],
    [(1, 3, 1), (1, 2, 1), (1, 1, 1)],
]
CHUNKS = [chunk for group in GROUPS for chunk in group]
SLOT = {chunk: i for i, chunk in enumerate(CHUNKS)}


def kernel(
    samples_total,
    r_hbm, c_hbm, g_hbm, e_ref,
    hamil_ref, corr_ref,
    rbuf, cbuf, gbuf, cw, rt, part, csend, crecv, xsend, xown, xrecv, ysend, yrecv,
    mown, mcore, mchip, mrecv, rmean, cmean,
    load_sem, rsend_sem, rrecv_sem, msend_sem, mrecv_sem,
    csend_sem, crecv_sem, xsend_sem, xrecv_sem, ysend_sem, yrecv_sem,
):
    w = lax.axis_index("walker")
    p = lax.axis_index("prow")
    q = lax.axis_index("pcol")
    x = w // 4
    yh = lax.rem(w // 2, 2)
    c = lax.rem(w, 2)
    samples, ncols = c_hbm.shape
    width = 2 * ncols

    def device(dx=0, dyh=0, dc=0, dp=0, dz=0):
        xx = lax.rem(x + dx, 4)
        yy = lax.rem(yh + dyh, 2)
        core = lax.rem(c + dc, 2)
        return {
            "walker": (xx * 2 + yy) * 2 + core,
            "prow": lax.rem(p + dp, 2),
            "pcol": lax.rem(q + dz, 4),
        }

    partners = [device(dc=1)]
    partners += [device(dx=a, dyh=b) for a in range(4) for b in range(2) if a or b]
    partners += [device(dp=a, dz=b) for a in range(2) for b in range(4) if a or b]
    partners += [device(dyh=1, dp=1)]
    barrier = pltpu.get_barrier_semaphore()
    for other in partners:
        pl.semaphore_signal(barrier, inc=1, device_id=other, device_id_type=MESH)

    loads = []
    for h in range(2):
        loads.append(pltpu.make_async_copy(
            r_hbm.at[:, pl.ds(128 * h, 128)], rbuf.at[h], load_sem.at[h]))
    loads.append(pltpu.make_async_copy(c_hbm, cbuf, load_sem.at[2]))
    loads.append(pltpu.make_async_copy(g_hbm, gbuf, load_sem.at[3]))
    for copy in loads:
        copy.start()
    pl.semaphore_wait(barrier, len(partners))

    started = []

    def send(src, dst, ssem, rsem, target):
        copy = pltpu.make_async_remote_copy(
            src_ref=src, dst_ref=dst, send_sem=ssem, recv_sem=rsem,
            device_id=target, device_id_type=MESH)
        copy.start()
        return copy

    piece = samples // 2

    def rows_of(i, k):
        return rbuf.at[i, pl.ds(piece * k, piece)]

    def send_rows(source, target, ks=(0, 1), dp=0, dz=0):
        i = SLOT[target]
        for k in ks:
            number = len(row_copies)
            if source is None:
                src = r_hbm.at[pl.ds(piece * k, piece), pl.ds(128 * target[2], 128)]
            else:
                src = rows_of(SLOT[source], k)
            row_copies.append(send(
                src, rows_of(i, k), rsend_sem.at[number], rrecv_sem.at[i, k], device(dp=dp, dz=dz)))

    row_copies = []

    def wait_piece(i, k):
        pltpu.make_async_remote_copy(
            src_ref=rows_of(i, k), dst_ref=rows_of(i, k), send_sem=rsend_sem.at[0], recv_sem=rrecv_sem.at[i, k],
            device_id=device(dz=1), device_id_type=MESH).wait_recv()

    waited = set()

    def wait_rows(*chunks, ks=(0, 1)):
        for chunk in chunks:
            for k in ks:
                if (chunk, k) not in waited:
                    waited.add((chunk, k))
                    wait_piece(SLOT[chunk], k)

    def send_own(up, down, across):
        for k in range(2):
            send_rows(None, (0, 3, up), (k,), dz=1)
            send_rows(None, (0, 1, down), (k,), dz=3)
            send_rows(None, (1, 0, across), (k,), dp=1)

    send_own(0, 1, 0)
    loads[0].wait()
    loads[1].wait()

    mown[...] = jnp.zeros_like(mown)

    def block_sums(ref, lanes):
        def body(i, acc):
            values = ref[pl.ds(pl.multiple_of(i * 128, 128), 128), :].astype(F32)
            return acc + jnp.sum(values.reshape(16, 8, lanes), axis=0)
        acc = lax.fori_loop(0, samples // 128, body, jnp.zeros((8, lanes), F32))
        return jnp.sum(acc, axis=0, keepdims=True)

    for h in range(2):
        mown[h:h + 1, :] = block_sums(rbuf.at[h], 128)
    loads[2].wait()
    csum = block_sums(cbuf, ncols)
    for k in range(ncols // 128):
        mown[2 + k:3 + k, :] = csum[:, 128 * k:128 * (k + 1)]

    copy = send(mown, mcore, msend_sem.at[0], mrecv_sem.at[0], device(dc=1))
    copy.wait_recv()
    started.append(copy)
    mchip[0] = mown[...] + mcore[...]
    copies = []
    for dx in range(4):
        for dyh in range(2):
            j = dx * 2 + dyh
            if j:
                copies.append(send(
                    mchip.at[0], mrecv.at[j], msend_sem.at[j], mrecv_sem.at[j], device(dx=dx, dyh=dyh)))
    send_own(1, 0, 1)
    loads[3].wait()
    total = mchip[0]
    for j, copy in enumerate(copies):
        copy.wait_recv()
        total = total + mrecv[j + 1]
    started += copies
    rmean[0, 0] = total * (1.0 / samples_total)
    mean_copies = []
    for a in range(2):
        for b in range(4):
            if a or b:
                j = 7 + a * 4 + b
                mean_copies.append(send(
                    rmean.at[0, 0], rmean.at[a, (4 - b) % 4],
                    msend_sem.at[j], mrecv_sem.at[j], device(dp=a, dz=b)))

    col_mean = jnp.concatenate([rmean[0, 0, 2 + k:3 + k, :] for k in range(ncols // 128)], axis=1)

    def build(i, _):
        rows = pl.ds(pl.multiple_of(i * 128, 128), 128)
        d_cols = (cbuf[rows, :].astype(F32) - col_mean).astype(BF16)
        cw[rows, pl.ds(0, ncols)] = d_cols
        energy = jnp.broadcast_to(e_ref[pl.ds(i, 1), :], (128, 128)).T
        energy = jnp.concatenate([energy] * (ncols // 128), axis=1)
        weighted = energy * d_cols.astype(F32) + gbuf[rows, :].astype(F32)
        cw[rows, pl.ds(ncols, ncols)] = weighted.astype(BF16)
        return 0

    lax.fori_loop(0, samples // 128, build, 0)

    half = 64
    mine = pl.ds(pl.multiple_of(half * c, half), half)
    other = pl.ds(pl.multiple_of(half * (1 - c), half), half)
    part_cols = [pl.ds(ncols * n, ncols) for n in range(2)]

    def core_copy(i, n):
        return pltpu.make_async_remote_copy(
            src_ref=csend.at[i, n], dst_ref=crecv.at[i, n], send_sem=csend_sem.at[i, n],
            recv_sem=crecv_sem.at[i, n], device_id=device(dc=1), device_id_type=MESH)

    def center(i):
        mean = cmean[i, 0:1, :]

        def body(k, _):
            rows = pl.ds(pl.multiple_of(k * 256, 256), 256)
            rt[rows, :] = (rbuf[i, rows, :].astype(F32) - mean).astype(BF16)
            return 0

        lax.fori_loop(0, samples // 256, body, 0)

    def product(cols):
        return lax.dot_general(
            rt[...], cw[:, cols], (((0,), (0,)), ((), ())), preferred_element_type=F32)

    def to_other_core(i, n):
        csend[i, n] = part[i, other, part_cols[n]].astype(BF16)
        core_copy(i, n).start()

    def multiply(i):
        center(i)
        part[i] = product(pl.ds(0, width))
        for n in range(2):
            to_other_core(i, n)

    def multiply_in_parts(i):
        center(i)
        for n in range(2):
            part[i, :, part_cols[n]] = product(part_cols[n])
            to_other_core(i, n)

    def multiply_group(group):
        first = SLOT[GROUPS[group][0]]

        def body(i, _):
            multiply(i)
            return 0

        lax.fori_loop(first, first + len(GROUPS[group]), body, 0)

    def x_target(i):
        return lax.rem(q + CHUNKS[i][1], 4)

    def x_copy(i, n):
        a, d, h = CHUNKS[i]
        hop = lax.rem(x_target(i) + 4 - x, 4)
        return pltpu.make_async_remote_copy(
            src_ref=xsend.at[i, n], dst_ref=xrecv.at[2 * a + h, hop - 1, n],
            send_sem=xsend_sem.at[i, n], recv_sem=xrecv_sem.at[2 * a + h, hop - 1, n],
            device_id=device(dx=hop), device_id_type=MESH)

    def chip_sum(i):
        a, d, h = CHUNKS[i]
        away = x_target(i) != x
        for n in range(2):
            core_copy(i, n).wait_recv()
            value = part[i, mine, part_cols[n]] + crecv[i, n].astype(F32)

            @pl.when(away)
            def _():
                xsend[i, n] = value.astype(BF16)
                x_copy(i, n).start()

            @pl.when(jnp.logical_not(away))
            def _():
                xown[2 * a + h, n] = value

    def y_copy(a, h, n):
        y = 2 * yh + p
        return pltpu.make_async_remote_copy(
            src_ref=ysend.at[2 * a + h, n], dst_ref=yrecv.at[y, n],
            send_sem=ysend_sem.at[2 * a + h, n], recv_sem=yrecv_sem.at[y, n],
            device_id=device(dyh=h + 2 - yh, dp=a), device_id_type=MESH)

    def x_sum(i):
        a, d, h = CHUNKS[i]
        row = 2 * a + h

        @pl.when(x_target(i) == x)
        def _():
            for n in range(2):
                value = xown[row, n]
                for hop in range(3):
                    pltpu.make_async_remote_copy(
                        src_ref=xsend.at[i, n], dst_ref=xrecv.at[row, hop, n],
                        send_sem=xsend_sem.at[i, n], recv_sem=xrecv_sem.at[row, hop, n],
                        device_id=device(dx=1), device_id_type=MESH).wait_recv()
                    value = value + xrecv[row, hop, n].astype(F32)
                if a == 0:
                    @pl.when(yh == h)
                    def _():
                        yrecv[2 * yh + p, n] = value.astype(BF16)

                    @pl.when(yh != h)
                    def _():
                        ysend[row, n] = value.astype(BF16)
                        y_copy(a, h, n).start()
                else:
                    ysend[row, n] = value.astype(BF16)
                    y_copy(a, h, n).start()

    def chip_sums(group):
        for chunk in GROUPS[group]:
            chip_sum(SLOT[chunk])

    def x_sums(group):
        for chunk in GROUPS[group]:
            x_sum(SLOT[chunk])

    count = len(CHUNKS)
    for h in range(2):
        cmean[SLOT[0, 0, h], 0:1, :] = rmean[0, 0, h:h + 1, :]
    multiply_group(0)
    for k in range(2):
        wait_rows((0, 3, 0), (0, 1, 1), ks=(k,))
        send_rows((0, 3, 0), (0, 2, 0), (k,), dz=1)
        send_rows((0, 1, 1), (0, 2, 1), (k,), dz=3)
    send_rows((0, 3, 0), (1, 3, 0), (1,), dp=1)
    wait_rows((1, 0, 0))
    send_rows((1, 0, 0), (1, 3, 0), (0,), dz=1)
    send_rows((1, 0, 0), (1, 1, 0), dz=3)
    chip_sums(0)
    for copy in mean_copies:
        copy.wait_recv()
    started += mean_copies
    for i, (a, d, h) in enumerate(CHUNKS):
        if (a, d) != (0, 0):
            cmean[i, 0:1, :] = rmean[a, d, h:h + 1, :]
    multiply_group(1)
    chip_sums(1)
    x_sums(0)
    wait_rows((1, 0, 1))
    send_rows((1, 0, 1), (1, 3, 1), dz=1)
    send_rows((1, 0, 1), (1, 1, 1), dz=3)
    wait_rows((0, 3, 1), (0, 1, 0))
    multiply_group(2)
    for k in range(2):
        for h in range(2):
            wait_rows((0, 2, h), ks=(k,))
            send_rows((0, 2, h), (1, 2, h), (k,), dp=1)
        if k == 0:
            chip_sums(2)
            x_sums(1)
    multiply_group(3)
    x_sums(2)
    chip_sums(3)
    for j, chunk in enumerate(GROUPS[4]):
        wait_rows(chunk)
        multiply(SLOT[chunk])
        if j == 1:
            x_sums(3)
        if j:
            chip_sum(SLOT[GROUPS[4][j - 1]])
    chip_sum(SLOT[GROUPS[4][2]])
    for chunk in GROUPS[5][:2]:
        wait_rows(chunk)
        multiply(SLOT[chunk])
    for chunk in GROUPS[5][:2]:
        chip_sum(SLOT[chunk])
    x_sums(4)
    wait_rows(GROUPS[5][2])
    multiply_in_parts(SLOT[GROUPS[5][2]])
    chip_sum(SLOT[GROUPS[5][2]])
    x_sums(5)

    for n, out in enumerate((corr_ref, hamil_ref)):
        for source in range(4):
            @pl.when(source != 2 * yh + p)
            def _(source=source, n=n):
                pltpu.make_async_remote_copy(
                    src_ref=ysend.at[0, n], dst_ref=yrecv.at[source, n],
                    send_sem=ysend_sem.at[0, n], recv_sem=yrecv_sem.at[source, n],
                    device_id=device(dp=1), device_id_type=MESH).wait_recv()
        for part_p in range(2):
            value = yrecv[part_p, n].astype(F32) + yrecv[2 + part_p, n].astype(F32)
            out[:, part_cols[part_p]] = value

    for copy in started + row_copies:
        copy.wait_send()
    for n in range(2):
        for i in range(count):
            core_copy(i, n).wait_send()

            @pl.when(x_target(i) != x)
            def _(i=i, n=n):
                x_copy(i, n).wait_send()
        for h in range(2):
            y_copy(1, h, n).wait_send()

            @pl.when(yh != h)
            def _(h=h, n=n):
                y_copy(0, h, n).wait_send()


def per_device(o_rows, o_cols, grad_energy, energy):
    samples, nrows = o_rows.shape
    ncols = o_cols.shape[1]
    width = 2 * ncols
    total = samples * lax.axis_size("walker")
    dma = pltpu.SemaphoreType.DMA
    out = jax.ShapeDtypeStruct((64, width), F32)
    hamil, corr = pl.pallas_call(
        functools.partial(kernel, total),
        name="tiles",
        out_shape=(out, out),
        in_specs=[pl.BlockSpec(memory_space=pl.ANY)] * 3 + [pl.BlockSpec(memory_space=pltpu.VMEM)],
        out_specs=(pl.BlockSpec(memory_space=pltpu.VMEM),) * 2,
        scratch_shapes=[
            pltpu.VMEM((16, samples, 128), BF16),
            pltpu.VMEM((samples, ncols), BF16),
            pltpu.VMEM((samples, ncols), BF16),
            pltpu.VMEM((samples, width), BF16),
            pltpu.VMEM((samples, 128), BF16),
            pltpu.VMEM((16, 128, width), F32),
            pltpu.VMEM((16, 2, 64, ncols), BF16),
            pltpu.VMEM((16, 2, 64, ncols), BF16),
            pltpu.VMEM((16, 2, 64, ncols), BF16),
            pltpu.VMEM((4, 2, 64, ncols), F32),
            pltpu.VMEM((4, 3, 2, 64, ncols), BF16),
            pltpu.VMEM((4, 2, 64, ncols), BF16),
            pltpu.VMEM((4, 2, 64, ncols), BF16),
            pltpu.VMEM((8, 128), F32),
            pltpu.VMEM((8, 128), F32),
            pltpu.VMEM((1, 8, 128), F32),
            pltpu.VMEM((8, 8, 128), F32),
            pltpu.VMEM((2, 4, 8, 128), F32),
            pltpu.VMEM((16, 8, 128), F32),
            dma((4,)), dma((28,)), dma((16, 2)), dma((15,)), dma((15,)),
            dma((16, 2)), dma((16, 2)), dma((16, 2)), dma((4, 3, 2)), dma((4, 2)), dma((4, 2)),
        ],
        compiler_params=pltpu.CompilerParams(
            collective_id=0, has_side_effects=True, vmem_limit_bytes=56 * 2**20),
        cost_estimate=pl.CostEstimate(
            flops=2 * samples * 2048 * width, bytes_accessed=6 * 2**20, transcendentals=0),
    )(o_rows, o_cols, grad_energy, energy.reshape(samples // 128, 128))
    scale = 1.0 / total
    return hamil * scale, corr * scale


def solution(mesh):
    in_specs = (
        P("walker", ("prow", "pcol")),
        P("walker", ("pcol", "prow")),
        P("walker", ("pcol", "prow")),
        P("walker"),
    )
    out_specs = (P(("prow", "walker"), "pcol"), P(("prow", "walker"), "pcol"))
    return jax.shard_map(
        per_device, mesh=mesh, in_specs=in_specs, out_specs=out_specs, check_vma=False
    )
```

```python
import functools

import jax
import jax.numpy as jnp
from jax import lax
from jax.experimental import pallas as pl
from jax.experimental.pallas import tpu as pltpu
from jax.sharding import PartitionSpec as P

MESH = pl.DeviceIdType.MESH
F32 = jnp.float32
BF16 = jnp.bfloat16

GROUPS = [
    [(0, 0, 0), (0, 0, 1)],
    [(0, 3, 0), (0, 1, 1), (1, 0, 0)],
    [(0, 3, 1), (0, 1, 0), (1, 0, 1)],
    [(0, 2, 0), (0, 2, 1)],
    [(1, 3, 0), (1, 1, 0)],
    [(1, 2, 0), (1, 3, 1), (1, 1, 1), (1, 2, 1)],
]
CHUNKS = [chunk for group in GROUPS for chunk in group]
SLOT = {chunk: i for i, chunk in enumerate(CHUNKS)}
HALVES = (0, 64, 128)
CUTS = {chunk: HALVES for chunk in CHUNKS}
CUTS[1, 3, 0] = CUTS[1, 1, 0] = (0, 43, 128)
CUTS[1, 3, 1] = CUTS[1, 1, 1] = (0, 86, 128)
CUTS[1, 2, 1] = (0, 43, 86, 128)


def kernel(
    samples_total,
    r_hbm, c_hbm, g_hbm, e_ref,
    hamil_ref, corr_ref,
    rbuf, cbuf, gbuf, cw, rt, part, csend, crecv, xsend, xown, xrecv, ysend, yrecv,
    mown, mcore, mchip, mrecv, rmean, cmean,
    load_sem, rsend_sem, rrecv_sem, msend_sem, mrecv_sem,
    csend_sem, crecv_sem, xsend_sem, xrecv_sem, ysend_sem, yrecv_sem,
):
    w = lax.axis_index("walker")
    p = lax.axis_index("prow")
    q = lax.axis_index("pcol")
    x = w // 4
    yh = lax.rem(w // 2, 2)
    c = lax.rem(w, 2)
    samples, ncols = c_hbm.shape
    width = 2 * ncols

    def device(dx=0, dyh=0, dc=0, dp=0, dz=0):
        xx = lax.rem(x + dx, 4)
        yy = lax.rem(yh + dyh, 2)
        core = lax.rem(c + dc, 2)
        return {
            "walker": (xx * 2 + yy) * 2 + core,
            "prow": lax.rem(p + dp, 2),
            "pcol": lax.rem(q + dz, 4),
        }

    partners = [device(dc=1)]
    partners += [device(dx=a, dyh=b) for a in range(4) for b in range(2) if a or b]
    partners += [device(dp=a, dz=b) for a in range(2) for b in range(4) if a or b]
    partners += [device(dyh=1, dp=1)]
    barrier = pltpu.get_barrier_semaphore()
    for other in partners:
        pl.semaphore_signal(barrier, inc=1, device_id=other, device_id_type=MESH)

    loads = []
    for h in range(2):
        loads.append(pltpu.make_async_copy(
            r_hbm.at[:, pl.ds(128 * h, 128)], rbuf.at[h], load_sem.at[h]))
    loads.append(pltpu.make_async_copy(c_hbm, cbuf, load_sem.at[2]))
    loads.append(pltpu.make_async_copy(g_hbm, gbuf, load_sem.at[3]))
    for copy in loads:
        copy.start()
    pl.semaphore_wait(barrier, len(partners))

    started = []

    def send(src, dst, ssem, rsem, target):
        copy = pltpu.make_async_remote_copy(
            src_ref=src, dst_ref=dst, send_sem=ssem, recv_sem=rsem,
            device_id=target, device_id_type=MESH)
        copy.start()
        return copy

    def span(chunk, k):
        unit = samples // 128
        low, high = CUTS[chunk][k], CUTS[chunk][k + 1]
        return pl.ds(low * unit, (high - low) * unit)

    def pieces(chunk):
        return range(len(CUTS[chunk]) - 1)

    def send_rows(source, target, ks=None, dp=0, dz=0):
        i = SLOT[target]
        for k in pieces(target) if ks is None else ks:
            number = len(row_copies)
            rows = span(target, k)
            if source is None:
                src = r_hbm.at[rows, pl.ds(128 * target[2], 128)]
            else:
                src = rbuf.at[SLOT[source], rows]
            row_copies.append(send(
                src, rbuf.at[i, rows], rsend_sem.at[number], rrecv_sem.at[i, k], device(dp=dp, dz=dz)))

    row_copies = []

    waited = set()

    def wait_rows(*chunks, ks=None):
        for chunk in chunks:
            for k in pieces(chunk) if ks is None else ks:
                if (chunk, k) not in waited:
                    waited.add((chunk, k))
                    rows = rbuf.at[SLOT[chunk], span(chunk, k)]
                    pltpu.make_async_remote_copy(
                        src_ref=rows, dst_ref=rows, send_sem=rsend_sem.at[0], recv_sem=rrecv_sem.at[SLOT[chunk], k],
                        device_id=device(dz=1), device_id_type=MESH).wait_recv()

    for h in range(2):
        for k in range(2):
            send_rows(None, (0, 3, h), (k,), dz=1)
            send_rows(None, (0, 1, 1 - h), (k,), dz=3)
            if h == 0:
                send_rows(None, (1, 0, 0), (k,), dp=1)
    loads[0].wait()
    loads[1].wait()

    mown[...] = jnp.zeros_like(mown)

    def block_sums(ref, lanes):
        def body(i, acc):
            values = ref[pl.ds(pl.multiple_of(i * 128, 128), 128), :].astype(F32)
            return acc + jnp.sum(values.reshape(16, 8, lanes), axis=0)
        acc = lax.fori_loop(0, samples // 128, body, jnp.zeros((8, lanes), F32))
        return jnp.sum(acc, axis=0, keepdims=True)

    for h in range(2):
        mown[h:h + 1, :] = block_sums(rbuf.at[h], 128)
    loads[2].wait()
    csum = block_sums(cbuf, ncols)
    for k in range(ncols // 128):
        mown[2 + k:3 + k, :] = csum[:, 128 * k:128 * (k + 1)]

    copy = send(mown, mcore, msend_sem.at[0], mrecv_sem.at[0], device(dc=1))
    copy.wait_recv()
    started.append(copy)
    mchip[0] = mown[...] + mcore[...]
    copies = []
    for dx in range(4):
        for dyh in range(2):
            j = dx * 2 + dyh
            if j:
                copies.append(send(
                    mchip.at[0], mrecv.at[j], msend_sem.at[j], mrecv_sem.at[j], device(dx=dx, dyh=dyh)))
    send_rows(None, (1, 0, 1), dp=1)
    loads[3].wait()
    total = mchip[0]
    for j, copy in enumerate(copies):
        copy.wait_recv()
        total = total + mrecv[j + 1]
    started += copies
    rmean[0, 0] = total * (1.0 / samples_total)
    mean_copies = []
    for a in range(2):
        for b in range(4):
            if a or b:
                j = 7 + a * 4 + b
                mean_copies.append(send(
                    rmean.at[0, 0], rmean.at[a, (4 - b) % 4],
                    msend_sem.at[j], mrecv_sem.at[j], device(dp=a, dz=b)))

    col_mean = jnp.concatenate([rmean[0, 0, 2 + k:3 + k, :] for k in range(ncols // 128)], axis=1)

    def build(i, _):
        rows = pl.ds(pl.multiple_of(i * 128, 128), 128)
        d_cols = (cbuf[rows, :].astype(F32) - col_mean).astype(BF16)
        cw[rows, pl.ds(0, ncols)] = d_cols
        energy = jnp.broadcast_to(e_ref[pl.ds(i, 1), :], (128, 128)).T
        energy = jnp.concatenate([energy] * (ncols // 128), axis=1)
        weighted = energy * d_cols.astype(F32) + gbuf[rows, :].astype(F32)
        cw[rows, pl.ds(ncols, ncols)] = weighted.astype(BF16)
        return 0

    lax.fori_loop(0, samples // 128, build, 0)

    half = 64
    mine = pl.ds(pl.multiple_of(half * c, half), half)
    other = pl.ds(pl.multiple_of(half * (1 - c), half), half)
    part_cols = [pl.ds(ncols * n, ncols) for n in range(2)]

    def core_copy(i, n):
        return pltpu.make_async_remote_copy(
            src_ref=csend.at[i, n], dst_ref=crecv.at[i, n], send_sem=csend_sem.at[i, n],
            recv_sem=crecv_sem.at[i, n], device_id=device(dc=1), device_id_type=MESH)

    def center(i, first=0, last=16):
        mean = cmean[i, 0:1, :]
        step = samples // 16

        def body(k, _):
            rows = pl.ds(pl.multiple_of(k * step, step), step)
            rt[rows, :] = (rbuf[i, rows, :].astype(F32) - mean).astype(BF16)
            return 0

        lax.fori_loop(first, last, body, 0)

    def to_other_core(i, n):
        csend[i, n] = part[i, other, part_cols[n]].astype(BF16)
        core_copy(i, n).start()

    def multiply(i):
        center(i)
        part[i] = lax.dot_general(
            rt[...], cw[...], (((0,), (0,)), ((), ())), preferred_element_type=F32)
        for n in range(2):
            to_other_core(i, n)

    def multiply_piece(chunk, k, first):
        i = SLOT[chunk]
        rows = span(chunk, k)
        values = (rbuf[i, rows, :].astype(F32) - cmean[i, 0:1, :]).astype(BF16)
        tile = lax.dot_general(
            values, cw[rows, :], (((0,), (0,)), ((), ())), preferred_element_type=F32)
        part[i] = tile if first else part[i] + tile

    def multiply_group(group):
        first = SLOT[GROUPS[group][0]]

        def body(i, _):
            multiply(i)
            return 0

        lax.fori_loop(first, first + len(GROUPS[group]), body, 0)

    def x_target(i):
        return lax.rem(q + CHUNKS[i][1], 4)

    def x_copy(i, n):
        a, d, h = CHUNKS[i]
        hop = lax.rem(x_target(i) + 4 - x, 4)
        return pltpu.make_async_remote_copy(
            src_ref=xsend.at[i, n], dst_ref=xrecv.at[2 * a + h, hop - 1, n],
            send_sem=xsend_sem.at[i, n], recv_sem=xrecv_sem.at[2 * a + h, hop - 1, n],
            device_id=device(dx=hop), device_id_type=MESH)

    def chip_sum(i):
        a, d, h = CHUNKS[i]
        away = x_target(i) != x
        for n in range(2):
            core_copy(i, n).wait_recv()
            value = part[i, mine, part_cols[n]] + crecv[i, n].astype(F32)

            @pl.when(away)
            def _():
                xsend[i, n] = value.astype(BF16)
                x_copy(i, n).start()

            @pl.when(jnp.logical_not(away))
            def _():
                xown[2 * a + h, n] = value

    def y_copy(a, h, n):
        y = 2 * yh + p
        return pltpu.make_async_remote_copy(
            src_ref=ysend.at[2 * a + h, n], dst_ref=yrecv.at[y, n],
            send_sem=ysend_sem.at[2 * a + h, n], recv_sem=yrecv_sem.at[y, n],
            device_id=device(dyh=h + 2 - yh, dp=a), device_id_type=MESH)

    def x_sum(i):
        a, d, h = CHUNKS[i]
        row = 2 * a + h

        @pl.when(x_target(i) == x)
        def _():
            for n in range(2):
                value = xown[row, n]
                for hop in range(3):
                    pltpu.make_async_remote_copy(
                        src_ref=xsend.at[i, n], dst_ref=xrecv.at[row, hop, n],
                        send_sem=xsend_sem.at[i, n], recv_sem=xrecv_sem.at[row, hop, n],
                        device_id=device(dx=1), device_id_type=MESH).wait_recv()
                    value = value + xrecv[row, hop, n].astype(F32)
                if a == 0:
                    @pl.when(yh == h)
                    def _():
                        yrecv[2 * yh + p, n] = value.astype(BF16)

                    @pl.when(yh != h)
                    def _():
                        ysend[row, n] = value.astype(BF16)
                        y_copy(a, h, n).start()
                else:
                    ysend[row, n] = value.astype(BF16)
                    y_copy(a, h, n).start()

    def chip_sums(group):
        for chunk in GROUPS[group]:
            chip_sum(SLOT[chunk])

    def x_sums(group):
        for chunk in GROUPS[group]:
            x_sum(SLOT[chunk])

    count = len(CHUNKS)
    for h in range(2):
        cmean[SLOT[0, 0, h], 0:1, :] = rmean[0, 0, h:h + 1, :]
    multiply_group(0)
    for k in range(2):
        wait_rows((0, 3, 0), (0, 1, 1), ks=(k,))
        send_rows((0, 3, 0), (0, 2, 0), (k,), dz=1)
        send_rows((0, 1, 1), (0, 2, 1), (k,), dz=3)
    send_rows((0, 3, 0), (1, 3, 0), (1,), dp=1)
    wait_rows((1, 0, 0))
    send_rows((1, 0, 0), (1, 3, 0), (0,), dz=1)
    send_rows((1, 0, 0), (1, 1, 0), (0,), dz=3)
    chip_sums(0)
    for copy in mean_copies:
        copy.wait_recv()
    started += mean_copies
    for i, (a, d, h) in enumerate(CHUNKS):
        if (a, d) != (0, 0):
            cmean[i, 0:1, :] = rmean[a, d, h:h + 1, :]
    multiply_group(1)
    chip_sums(1)
    x_sums(0)
    wait_rows((1, 0, 1))
    send_rows((1, 0, 1), (1, 3, 1), dz=1)
    send_rows((1, 0, 1), (1, 1, 1), dz=3)
    wait_rows((0, 3, 1), (0, 1, 0))
    send_rows((0, 1, 0), (1, 1, 0), (1,), dp=1)
    multiply_group(2)
    wait_rows((0, 2, 0), ks=(0,))
    send_rows((0, 2, 0), (1, 2, 0), (0,), dp=1)
    chip_sums(2)
    x_sums(1)
    wait_rows((0, 2, 0), (0, 2, 1))
    send_rows((0, 2, 0), (1, 2, 0), (1,), dp=1)
    send_rows((0, 2, 1), (1, 2, 1), (2,), dp=1)
    multiply_group(3)
    x_sums(2)
    chip_sums(3)
    for chunk in GROUPS[4]:
        wait_rows(chunk)
        multiply(SLOT[chunk])
    chip_sums(4)
    wait_rows((1, 3, 1), ks=(0,))
    send_rows((1, 3, 1), (1, 2, 1), (0,), dz=1)
    wait_rows((1, 1, 1), ks=(0,))
    send_rows((1, 1, 1), (1, 2, 1), (1,), dz=3)
    multiply_piece((1, 3, 1), 0, True)
    multiply_piece((1, 1, 1), 0, True)
    x_sums(3)
    for chunk in GROUPS[5][:3]:
        wait_rows(chunk)
        if chunk == (1, 2, 0):
            multiply(SLOT[chunk])
        else:
            multiply_piece(chunk, 1, False)
            for n in range(2):
                to_other_core(SLOT[chunk], n)
    for chunk in GROUPS[5][:3]:
        chip_sum(SLOT[chunk])
    last = (1, 2, 1)
    for k in (2, 0, 1):
        wait_rows(last, ks=(k,))
        multiply_piece(last, k, k == 2)
    for n in range(2):
        to_other_core(SLOT[last], n)
    x_sums(4)
    chip_sum(SLOT[last])
    x_sums(5)

    for n, out in enumerate((corr_ref, hamil_ref)):
        for source in range(4):
            @pl.when(source != 2 * yh + p)
            def _(source=source, n=n):
                pltpu.make_async_remote_copy(
                    src_ref=ysend.at[0, n], dst_ref=yrecv.at[source, n],
                    send_sem=ysend_sem.at[0, n], recv_sem=yrecv_sem.at[source, n],
                    device_id=device(dp=1), device_id_type=MESH).wait_recv()
        for part_p in range(2):
            value = yrecv[part_p, n].astype(F32) + yrecv[2 + part_p, n].astype(F32)
            out[:, part_cols[part_p]] = value

    for copy in started + row_copies:
        copy.wait_send()
    for n in range(2):
        for i in range(count):
            core_copy(i, n).wait_send()

            @pl.when(x_target(i) != x)
            def _(i=i, n=n):
                x_copy(i, n).wait_send()
        for h in range(2):
            y_copy(1, h, n).wait_send()

            @pl.when(yh != h)
            def _(h=h, n=n):
                y_copy(0, h, n).wait_send()


def per_device(o_rows, o_cols, grad_energy, energy):
    samples, nrows = o_rows.shape
    ncols = o_cols.shape[1]
    width = 2 * ncols
    total = samples * lax.axis_size("walker")
    dma = pltpu.SemaphoreType.DMA
    out = jax.ShapeDtypeStruct((64, width), F32)
    hamil, corr = pl.pallas_call(
        functools.partial(kernel, total),
        name="tiles",
        out_shape=(out, out),
        in_specs=[pl.BlockSpec(memory_space=pl.ANY)] * 3 + [pl.BlockSpec(memory_space=pltpu.VMEM)],
        out_specs=(pl.BlockSpec(memory_space=pltpu.VMEM),) * 2,
        scratch_shapes=[
            pltpu.VMEM((16, samples, 128), BF16),
            pltpu.VMEM((samples, ncols), BF16),
            pltpu.VMEM((samples, ncols), BF16),
            pltpu.VMEM((samples, width), BF16),
            pltpu.VMEM((samples, 128), BF16),
            pltpu.VMEM((16, 128, width), F32),
            pltpu.VMEM((16, 2, 64, ncols), BF16),
            pltpu.VMEM((16, 2, 64, ncols), BF16),
            pltpu.VMEM((16, 2, 64, ncols), BF16),
            pltpu.VMEM((4, 2, 64, ncols), F32),
            pltpu.VMEM((4, 3, 2, 64, ncols), BF16),
            pltpu.VMEM((4, 2, 64, ncols), BF16),
            pltpu.VMEM((4, 2, 64, ncols), BF16),
            pltpu.VMEM((8, 128), F32),
            pltpu.VMEM((8, 128), F32),
            pltpu.VMEM((1, 8, 128), F32),
            pltpu.VMEM((8, 8, 128), F32),
            pltpu.VMEM((2, 4, 8, 128), F32),
            pltpu.VMEM((16, 8, 128), F32),
            dma((4,)), dma((30,)), dma((16, 3)), dma((15,)), dma((15,)),
            dma((16, 2)), dma((16, 2)), dma((16, 2)), dma((4, 3, 2)), dma((4, 2)), dma((4, 2)),
        ],
        compiler_params=pltpu.CompilerParams(
            collective_id=0, has_side_effects=True, vmem_limit_bytes=56 * 2**20),
        cost_estimate=pl.CostEstimate(
            flops=2 * samples * 2048 * width, bytes_accessed=6 * 2**20, transcendentals=0),
    )(o_rows, o_cols, grad_energy, energy.reshape(samples // 128, 128))
    scale = 1.0 / total
    return hamil * scale, corr * scale


def solution(mesh):
    in_specs = (
        P("walker", ("prow", "pcol")),
        P("walker", ("pcol", "prow")),
        P("walker", ("pcol", "prow")),
        P("walker"),
    )
    out_specs = (P(("prow", "walker"), "pcol"), P(("prow", "walker"), "pcol"))
    return jax.shard_map(
        per_device, mesh=mesh, in_specs=in_specs, out_specs=out_specs, check_vma=False
    )
```

```python
import functools

import jax
import jax.numpy as jnp
from jax import lax
from jax.experimental import pallas as pl
from jax.experimental.pallas import tpu as pltpu
from jax.sharding import PartitionSpec as P

MESH = pl.DeviceIdType.MESH
F32 = jnp.float32
BF16 = jnp.bfloat16

GROUPS = [
    [(0, 0, 0), (0, 0, 1)],
    [(0, 3, 0), (0, 1, 1), (1, 0, 0)],
    [(0, 3, 1), (0, 1, 0), (1, 0, 1)],
    [(0, 2, 0), (0, 2, 1)],
    [(1, 3, 0), (1, 1, 0)],
    [(1, 2, 0), (1, 3, 1), (1, 1, 1), (1, 2, 1)],
]
CHUNKS = [chunk for group in GROUPS for chunk in group]
SLOT = {chunk: i for i, chunk in enumerate(CHUNKS)}
HALVES = (0, 64, 128)
CUTS = {chunk: HALVES for chunk in CHUNKS}
CUTS[1, 3, 0] = CUTS[1, 1, 0] = (0, 43, 128)
CUTS[1, 3, 1] = CUTS[1, 1, 1] = (0, 86, 128)
CUTS[1, 2, 1] = (0, 43, 86, 128)


def kernel(
    samples_total,
    r_hbm, c_hbm, g_hbm, e_ref,
    hamil_ref, corr_ref,
    rbuf, cbuf, gbuf, cw, rt, part, csend, crecv, xsend, xown, xrecv, ysend, yrecv,
    mown, mcore, mchip, mrecv, rmean, cmean, result,
    load_sem, rsend_sem, rrecv_sem, msend_sem, mrecv_sem,
    csend_sem, crecv_sem, xsend_sem, xrecv_sem, ysend_sem, yrecv_sem,
):
    w = lax.axis_index("walker")
    p = lax.axis_index("prow")
    q = lax.axis_index("pcol")
    x = w // 4
    yh = lax.rem(w // 2, 2)
    c = lax.rem(w, 2)
    samples, ncols = c_hbm.shape
    width = 2 * ncols

    def device(dx=0, dyh=0, dc=0, dp=0, dz=0):
        xx = lax.rem(x + dx, 4)
        yy = lax.rem(yh + dyh, 2)
        core = lax.rem(c + dc, 2)
        return {
            "walker": (xx * 2 + yy) * 2 + core,
            "prow": lax.rem(p + dp, 2),
            "pcol": lax.rem(q + dz, 4),
        }

    partners = [device(dc=1)]
    partners += [device(dx=a, dyh=b) for a in range(4) for b in range(2) if a or b]
    partners += [device(dp=a, dz=b) for a in range(2) for b in range(4) if a or b]
    partners += [device(dyh=1, dp=1)]
    barrier = pltpu.get_barrier_semaphore()
    for other in partners:
        pl.semaphore_signal(barrier, inc=1, device_id=other, device_id_type=MESH)

    loads = []
    for h in range(2):
        loads.append(pltpu.make_async_copy(
            r_hbm.at[:, pl.ds(128 * h, 128)], rbuf.at[h], load_sem.at[h]))
    loads.append(pltpu.make_async_copy(c_hbm, cbuf, load_sem.at[2]))
    loads.append(pltpu.make_async_copy(g_hbm, gbuf, load_sem.at[3]))
    for copy in loads:
        copy.start()
    pl.semaphore_wait(barrier, len(partners))

    started = []

    def send(src, dst, ssem, rsem, target):
        copy = pltpu.make_async_remote_copy(
            src_ref=src, dst_ref=dst, send_sem=ssem, recv_sem=rsem,
            device_id=target, device_id_type=MESH)
        copy.start()
        return copy

    def span(chunk, k):
        unit = samples // 128
        low, high = CUTS[chunk][k], CUTS[chunk][k + 1]
        return pl.ds(low * unit, (high - low) * unit)

    def pieces(chunk):
        return range(len(CUTS[chunk]) - 1)

    def send_rows(source, target, ks=None, dp=0, dz=0):
        i = SLOT[target]
        for k in pieces(target) if ks is None else ks:
            number = len(row_copies)
            rows = span(target, k)
            if source is None:
                src = r_hbm.at[rows, pl.ds(128 * target[2], 128)]
            else:
                src = rbuf.at[SLOT[source], rows]
            row_copies.append(send(
                src, rbuf.at[i, rows], rsend_sem.at[number], rrecv_sem.at[i, k], device(dp=dp, dz=dz)))

    row_copies = []

    waited = set()

    def wait_rows(*chunks, ks=None):
        for chunk in chunks:
            for k in pieces(chunk) if ks is None else ks:
                if (chunk, k) not in waited:
                    waited.add((chunk, k))
                    rows = rbuf.at[SLOT[chunk], span(chunk, k)]
                    pltpu.make_async_remote_copy(
                        src_ref=rows, dst_ref=rows, send_sem=rsend_sem.at[0], recv_sem=rrecv_sem.at[SLOT[chunk], k],
                        device_id=device(dz=1), device_id_type=MESH).wait_recv()

    for h in range(2):
        for k in range(2):
            send_rows(None, (0, 3, h), (k,), dz=1)
            send_rows(None, (0, 1, 1 - h), (k,), dz=3)
            if h == 0:
                send_rows(None, (1, 0, 0), (k,), dp=1)
    loads[0].wait()
    loads[1].wait()

    mown[...] = jnp.zeros_like(mown)

    def block_sums(ref, lanes):
        def body(i, acc):
            values = ref[pl.ds(pl.multiple_of(i * 128, 128), 128), :].astype(F32)
            return acc + jnp.sum(values.reshape(16, 8, lanes), axis=0)
        acc = lax.fori_loop(0, samples // 128, body, jnp.zeros((8, lanes), F32))
        return jnp.sum(acc, axis=0, keepdims=True)

    for h in range(2):
        mown[h:h + 1, :] = block_sums(rbuf.at[h], 128)
    loads[2].wait()
    csum = block_sums(cbuf, ncols)
    for k in range(ncols // 128):
        mown[2 + k:3 + k, :] = csum[:, 128 * k:128 * (k + 1)]

    copy = send(mown, mcore, msend_sem.at[0], mrecv_sem.at[0], device(dc=1))
    copy.wait_recv()
    started.append(copy)
    mchip[0] = mown[...] + mcore[...]
    copies = []
    for dx in range(4):
        for dyh in range(2):
            j = dx * 2 + dyh
            if j:
                copies.append(send(
                    mchip.at[0], mrecv.at[j], msend_sem.at[j], mrecv_sem.at[j], device(dx=dx, dyh=dyh)))
    send_rows(None, (1, 0, 1), dp=1)
    loads[3].wait()
    total = mchip[0]
    for j, copy in enumerate(copies):
        copy.wait_recv()
        total = total + mrecv[j + 1]
    started += copies
    rmean[0, 0] = total * (1.0 / samples_total)
    mean_copies = []
    for a in range(2):
        for b in range(4):
            if a or b:
                j = 7 + a * 4 + b
                mean_copies.append(send(
                    rmean.at[0, 0], rmean.at[a, (4 - b) % 4],
                    msend_sem.at[j], mrecv_sem.at[j], device(dp=a, dz=b)))

    col_mean = jnp.concatenate([rmean[0, 0, 2 + k:3 + k, :] for k in range(ncols // 128)], axis=1)

    def build(i, _):
        rows = pl.ds(pl.multiple_of(i * 128, 128), 128)
        d_cols = (cbuf[rows, :].astype(F32) - col_mean).astype(BF16)
        cw[rows, pl.ds(0, ncols)] = d_cols
        energy = jnp.broadcast_to(e_ref[pl.ds(i, 1), :], (128, 128)).T
        energy = jnp.concatenate([energy] * (ncols // 128), axis=1)
        weighted = energy * d_cols.astype(F32) + gbuf[rows, :].astype(F32)
        cw[rows, pl.ds(ncols, ncols)] = weighted.astype(BF16)
        return 0

    lax.fori_loop(0, samples // 128, build, 0)

    half = 64
    mine = pl.ds(pl.multiple_of(half * c, half), half)
    other = pl.ds(pl.multiple_of(half * (1 - c), half), half)
    part_cols = [pl.ds(ncols * n, ncols) for n in range(2)]

    def core_copy(i, n):
        return pltpu.make_async_remote_copy(
            src_ref=csend.at[i, n], dst_ref=crecv.at[i, n], send_sem=csend_sem.at[i, n],
            recv_sem=crecv_sem.at[i, n], device_id=device(dc=1), device_id_type=MESH)

    def center(i, first=0, last=16):
        mean = cmean[i, 0:1, :]
        step = samples // 16

        def body(k, _):
            rows = pl.ds(pl.multiple_of(k * step, step), step)
            rt[rows, :] = (rbuf[i, rows, :].astype(F32) - mean).astype(BF16)
            return 0

        lax.fori_loop(first, last, body, 0)

    def to_other_core(i, n):
        csend[i, n] = part[i, other, part_cols[n]].astype(BF16)
        core_copy(i, n).start()

    def multiply(i):
        center(i)
        part[i] = lax.dot_general(
            rt[...], cw[...], (((0,), (0,)), ((), ())), preferred_element_type=F32)
        for n in range(2):
            to_other_core(i, n)

    def multiply_piece(chunk, k, first):
        i = SLOT[chunk]
        rows = span(chunk, k)
        values = (rbuf[i, rows, :].astype(F32) - cmean[i, 0:1, :]).astype(BF16)
        tile = lax.dot_general(
            values, cw[rows, :], (((0,), (0,)), ((), ())), preferred_element_type=F32)
        part[i] = tile if first else part[i] + tile

    def multiply_group(group):
        first = SLOT[GROUPS[group][0]]

        def body(i, _):
            multiply(i)
            return 0

        lax.fori_loop(first, first + len(GROUPS[group]), body, 0)

    def x_target(i):
        return lax.rem(q + CHUNKS[i][1], 4)

    def x_copy(i, n):
        a, d, h = CHUNKS[i]
        hop = lax.rem(x_target(i) + 4 - x, 4)
        return pltpu.make_async_remote_copy(
            src_ref=xsend.at[i, n], dst_ref=xrecv.at[2 * a + h, hop - 1, n],
            send_sem=xsend_sem.at[i, n], recv_sem=xrecv_sem.at[2 * a + h, hop - 1, n],
            device_id=device(dx=hop), device_id_type=MESH)

    def chip_sum(i):
        a, d, h = CHUNKS[i]
        away = x_target(i) != x
        for n in range(2):
            core_copy(i, n).wait_recv()
            value = part[i, mine, part_cols[n]] + crecv[i, n].astype(F32)

            @pl.when(away)
            def _():
                xsend[i, n] = value.astype(BF16)
                x_copy(i, n).start()

            @pl.when(jnp.logical_not(away))
            def _():
                xown[2 * a + h, n] = value

    def y_copy(a, h, n):
        y = 2 * yh + p
        return pltpu.make_async_remote_copy(
            src_ref=ysend.at[2 * a + h, n], dst_ref=yrecv.at[y, n],
            send_sem=ysend_sem.at[2 * a + h, n], recv_sem=yrecv_sem.at[y, n],
            device_id=device(dyh=h + 2 - yh, dp=a), device_id_type=MESH)

    def x_sum(i):
        a, d, h = CHUNKS[i]
        row = 2 * a + h

        @pl.when(x_target(i) == x)
        def _():
            for n in range(2):
                value = xown[row, n]
                for hop in range(3):
                    pltpu.make_async_remote_copy(
                        src_ref=xsend.at[i, n], dst_ref=xrecv.at[row, hop, n],
                        send_sem=xsend_sem.at[i, n], recv_sem=xrecv_sem.at[row, hop, n],
                        device_id=device(dx=1), device_id_type=MESH).wait_recv()
                    value = value + xrecv[row, hop, n].astype(F32)
                if a == 0:
                    @pl.when(yh == h)
                    def _():
                        yrecv[2 * yh + p, n] = value.astype(BF16)

                    @pl.when(yh != h)
                    def _():
                        ysend[row, n] = value.astype(BF16)
                        y_copy(a, h, n).start()
                else:
                    ysend[row, n] = value.astype(BF16)
                    y_copy(a, h, n).start()

    def chip_sums(group):
        for chunk in GROUPS[group]:
            chip_sum(SLOT[chunk])

    def x_sums(group):
        for chunk in GROUPS[group]:
            x_sum(SLOT[chunk])

    count = len(CHUNKS)
    for h in range(2):
        cmean[SLOT[0, 0, h], 0:1, :] = rmean[0, 0, h:h + 1, :]
    multiply_group(0)
    for k in range(2):
        wait_rows((0, 3, 0), (0, 1, 1), ks=(k,))
        send_rows((0, 3, 0), (0, 2, 0), (k,), dz=1)
        send_rows((0, 1, 1), (0, 2, 1), (k,), dz=3)
    send_rows((0, 3, 0), (1, 3, 0), (1,), dp=1)
    wait_rows((1, 0, 0))
    send_rows((1, 0, 0), (1, 3, 0), (0,), dz=1)
    send_rows((1, 0, 0), (1, 1, 0), (0,), dz=3)
    chip_sums(0)
    for copy in mean_copies:
        copy.wait_recv()
    started += mean_copies
    for i, (a, d, h) in enumerate(CHUNKS):
        if (a, d) != (0, 0):
            cmean[i, 0:1, :] = rmean[a, d, h:h + 1, :]
    multiply_group(1)
    chip_sums(1)
    x_sums(0)
    wait_rows((1, 0, 1))
    send_rows((1, 0, 1), (1, 3, 1), dz=1)
    send_rows((1, 0, 1), (1, 1, 1), dz=3)
    wait_rows((0, 3, 1), (0, 1, 0))
    send_rows((0, 1, 0), (1, 1, 0), (1,), dp=1)
    multiply_group(2)
    wait_rows((0, 2, 0), ks=(0,))
    send_rows((0, 2, 0), (1, 2, 0), (0,), dp=1)
    chip_sums(2)
    x_sums(1)
    wait_rows((0, 2, 0), (0, 2, 1))
    send_rows((0, 2, 0), (1, 2, 0), (1,), dp=1)
    send_rows((0, 2, 1), (1, 2, 1), (2,), dp=1)
    multiply_group(3)
    x_sums(2)
    chip_sums(3)
    for chunk in GROUPS[4]:
        wait_rows(chunk)
        multiply(SLOT[chunk])
    chip_sums(4)
    wait_rows((1, 3, 1), ks=(0,))
    send_rows((1, 3, 1), (1, 2, 1), (0,), dz=1)
    wait_rows((1, 1, 1), ks=(0,))
    send_rows((1, 1, 1), (1, 2, 1), (1,), dz=3)
    multiply_piece((1, 3, 1), 0, True)
    multiply_piece((1, 1, 1), 0, True)
    x_sums(3)
    for chunk in GROUPS[5][:3]:
        wait_rows(chunk)
        if chunk == (1, 2, 0):
            multiply(SLOT[chunk])
        else:
            multiply_piece(chunk, 1, False)
            for n in range(2):
                to_other_core(SLOT[chunk], n)
    for chunk in GROUPS[5][:3]:
        chip_sum(SLOT[chunk])
    last = (1, 2, 1)
    for k in (2, 0, 1):
        wait_rows(last, ks=(k,))
        multiply_piece(last, k, k == 2)
    for n in range(2):
        to_other_core(SLOT[last], n)
    x_sums(4)
    chip_sum(SLOT[last])
    x_sums(5)

    out_copies = []
    for n, out in enumerate((corr_ref, hamil_ref)):
        for source in range(4):
            @pl.when(source != 2 * yh + p)
            def _(source=source, n=n):
                pltpu.make_async_remote_copy(
                    src_ref=ysend.at[0, n], dst_ref=yrecv.at[source, n],
                    send_sem=ysend_sem.at[0, n], recv_sem=yrecv_sem.at[source, n],
                    device_id=device(dp=1), device_id_type=MESH).wait_recv()
        for part_p in range(2):
            value = yrecv[part_p, n].astype(F32) + yrecv[2 + part_p, n].astype(F32)
            result[n, :, part_cols[part_p]] = value
        out_copies.append(pltpu.make_async_copy(result.at[n], out, load_sem.at[n]))
        out_copies[n].start()

    for copy in out_copies:
        copy.wait()
    for copy in started + row_copies:
        copy.wait_send()
    for n in range(2):
        for i in range(count):
            core_copy(i, n).wait_send()

            @pl.when(x_target(i) != x)
            def _(i=i, n=n):
                x_copy(i, n).wait_send()
        for h in range(2):
            y_copy(1, h, n).wait_send()

            @pl.when(yh != h)
            def _(h=h, n=n):
                y_copy(0, h, n).wait_send()


def per_device(o_rows, o_cols, grad_energy, energy):
    samples, nrows = o_rows.shape
    ncols = o_cols.shape[1]
    width = 2 * ncols
    total = samples * lax.axis_size("walker")
    dma = pltpu.SemaphoreType.DMA
    out = jax.ShapeDtypeStruct((64, width), F32)
    hamil, corr = pl.pallas_call(
        functools.partial(kernel, total),
        name="tiles",
        out_shape=(out, out),
        in_specs=[pl.BlockSpec(memory_space=pl.ANY)] * 3 + [pl.BlockSpec(memory_space=pltpu.VMEM)],
        out_specs=(pl.BlockSpec(memory_space=pl.ANY),) * 2,
        scratch_shapes=[
            pltpu.VMEM((16, samples, 128), BF16),
            pltpu.VMEM((samples, ncols), BF16),
            pltpu.VMEM((samples, ncols), BF16),
            pltpu.VMEM((samples, width), BF16),
            pltpu.VMEM((samples, 128), BF16),
            pltpu.VMEM((16, 128, width), F32),
            pltpu.VMEM((16, 2, 64, ncols), BF16),
            pltpu.VMEM((16, 2, 64, ncols), BF16),
            pltpu.VMEM((16, 2, 64, ncols), BF16),
            pltpu.VMEM((4, 2, 64, ncols), F32),
            pltpu.VMEM((4, 3, 2, 64, ncols), BF16),
            pltpu.VMEM((4, 2, 64, ncols), BF16),
            pltpu.VMEM((4, 2, 64, ncols), BF16),
            pltpu.VMEM((8, 128), F32),
            pltpu.VMEM((8, 128), F32),
            pltpu.VMEM((1, 8, 128), F32),
            pltpu.VMEM((8, 8, 128), F32),
            pltpu.VMEM((2, 4, 8, 128), F32),
            pltpu.VMEM((16, 8, 128), F32),
            pltpu.VMEM((2, 64, width), F32),
            dma((4,)), dma((30,)), dma((16, 3)), dma((15,)), dma((15,)),
            dma((16, 2)), dma((16, 2)), dma((16, 2)), dma((4, 3, 2)), dma((4, 2)), dma((4, 2)),
        ],
        compiler_params=pltpu.CompilerParams(
            collective_id=0, has_side_effects=True, vmem_limit_bytes=int(53.5 * 2**20)),
        cost_estimate=pl.CostEstimate(
            flops=2 * samples * 2048 * width, bytes_accessed=6 * 2**20, transcendentals=0),
    )(o_rows, o_cols, grad_energy, energy.reshape(samples // 128, 128))
    scale = 1.0 / total
    return hamil * scale, corr * scale


def solution(mesh):
    in_specs = (
        P("walker", ("prow", "pcol")),
        P("walker", ("pcol", "prow")),
        P("walker", ("pcol", "prow")),
        P("walker"),
    )
    out_specs = (P(("prow", "walker"), "pcol"), P(("prow", "walker"), "pcol"))
    return jax.shard_map(
        per_device, mesh=mesh, in_specs=in_specs, out_specs=out_specs, check_vma=False
    )
```
